256 devices in a mesh: row: 8 (over x, y_lo), col: 32 (over z, y_hi, core).
Axes of the slice: x: 4, y: 4 (y_hi: 2, y_lo: 2; y = y_hi * 2 + y_lo), z: 8, core: 2. Of those that a mesh axis runs over, the one named last changes fastest.
Arguments:
- hidden_in: bfloat16 [64, 256, 384], P('row', 'col'), may hold values from -6 to 6
- skip_input: bfloat16 [64, 256, 384], P('row', 'col'), may hold values from -6 to 6
- cache_frames: bfloat16 [2, 64, 256, 384], P(None, 'row', 'col'), may hold values from -3 to 3
- norm_gain: float32 [384], replicated, may hold values from 0.1 to 1.9
- conv_weight: bfloat16 [27, 384, 384], replicated, may hold values from -0.0625 to 0.0625
- conv_bias: float32 [384], replicated, may hold values from -3 to 3
- attn_gain: float32 [384], replicated, may hold values from 0.1 to 1.9
- w_qkv: bfloat16 [384, 1152], replicated, may hold values from -1 to 1
- b_qkv: float32 [1152], replicated, may hold values from -3 to 3
- w_proj: bfloat16 [384, 384], replicated, may hold values from -0.3125 to 0.3125
- b_proj: float32 [384], replicated, may hold values from -3 to 3
Outputs:
- block_out: bfloat16 [64, 256, 384], P('row', 'col')
The draws below stay inside these ranges and needn't reach their ends.
All inputs are finite; a program needn't handle non-finite values.
Results may differ from the reference program's by a relative error of at most 0.02.
Values may be sent and summed in bfloat16 or wider, within the bound.
No kernel may reach another device: no remote copies, remote signals or barrier semaphores. Data moves between devices by JAX's collectives and lax.ppermute only.
A program may use at most 128 MiB of HBM per device.

```python
import math
import jax
import jax.numpy as jnp
from jax import lax

C = 384
NH = 64
NW = 256


def draw_w_qkv(key, part):
    key = jax.random.fold_in(key, 11)
    first, second, third = jax.random.split(key, 3)
    spread = C ** (-0.5)
    w_query = jax.random.normal(first, (C, C), jnp.float32) * spread * 2.0
    w_key = jax.random.normal(second, (C, C), jnp.float32) * spread * 2.0
    w_value = jax.random.normal(third, (C, C), jnp.float32) * spread
    joined = jnp.concatenate([w_query, w_key, w_value], axis=1)
    return jnp.clip(joined, -1.0, 1.0).astype(jnp.bfloat16)


def level_of(own_key, dims, pieces, smallest, top_value):
    gain, own = 1.0, jax.random.fold_in(own_key, 6)
    for dim, blocks in pieces:
        heights = jnp.exp(jax.random.uniform(jax.random.fold_in(own, dim), (blocks,), jnp.float32, smallest / len(pieces), top_value / len(pieces)))
        gain = gain * jnp.repeat(heights, dims[dim] // blocks).reshape([-1 if axis == dim else 1 for axis in range(len(dims))])
    return gain


def centred(stream_key, shape, width, limit, shards=(), dtype=jnp.bfloat16):
    factor_of = level_of(stream_key, shape, shards, -0.22, 0.18) if shards else 1.0
    values = jax.random.normal(stream_key, shape, jnp.float32) * width * factor_of
    return jnp.minimum(jnp.maximum(values, -limit), limit).astype(dtype)


def setup_inputs(seed: int = 0) -> dict:
    key_list = jax.random.split(jax.random.key(seed), 12)
    return {
        "hidden_in": centred(key_list[0], (NH, NW, C), 1.0, 6.0, ((0, 8), (1, 32))),
        "skip_input": centred(key_list[1], (NH, NW, C), 1.0, 6.0, ((0, 8), (1, 32))),
        "cache_frames": centred(key_list[2], (2, NH, NW, C), 0.5, 3.0, ((1, 8), (2, 32))),
        "norm_gain": jnp.clip(1.0 + 0.18 * jax.random.normal(key_list[3], (C,), jnp.float32), 0.1, 1.9),
        "conv_weight": centred(key_list[4], (27, C, C), (27 * C) ** -0.5, 0.0625),
        "conv_bias": centred(key_list[5], (C,), 0.5, 3.0, (), jnp.float32),
        "attn_gain": jnp.clip(1.0 + 0.18 * jax.random.normal(key_list[6], (C,), jnp.float32), 0.1, 1.9),
        "w_qkv": draw_w_qkv(jax.random.fold_in(key_list[11], 71), 0),
        "b_qkv": centred(key_list[8], (3 * C,), 0.5, 3.0, (), jnp.float32),
        "w_proj": centred(key_list[9], (C, C), C ** -0.5, 0.3125),
        "b_proj": centred(key_list[10], (C,), 0.5, 3.0, (), jnp.float32),
    }


def rms_scale(values_in, gain_vec):
    floats = values_in.astype(jnp.float32)
    return floats * lax.rsqrt(lax.optimization_barrier(jnp.mean(floats * floats, axis=-1, keepdims=True)) + 1e-06) * gain_vec

def reference(hidden_in, skip_input, cache_frames, norm_gain, conv_weight, conv_bias, attn_gain, w_qkv, b_qkv, w_proj, b_proj):
    frame_rows, frame_cols, channels = hidden_in.shape
    conv_in = jax.nn.silu(rms_scale(hidden_in, norm_gain)).astype(jnp.bfloat16)
    frames_in = jnp.concatenate([cache_frames, conv_in[None]], axis=0)
    padded = jnp.pad(frames_in, ((0, 0), (1, 1), (1, 1), (0, 0)))
    conv_sum = jnp.zeros((frame_rows * frame_cols, channels), jnp.float32) + conv_bias
    for frame_idx in range(3):
        for shift_row in range(3):
            for shift_col in range(3):
                window = padded[frame_idx, shift_row:shift_row + frame_rows, shift_col:shift_col + frame_cols]
                conv_sum = conv_sum + jnp.dot(window.reshape(-1, channels), conv_weight[9 * frame_idx + 3 * shift_row + shift_col], preferred_element_type=jnp.float32)
    middle = (skip_input.reshape(-1, channels).astype(jnp.float32) + conv_sum).astype(jnp.bfloat16)
    normed = rms_scale(middle, attn_gain).astype(jnp.bfloat16)
    projected = jnp.dot(normed, w_qkv, preferred_element_type=jnp.float32) + b_qkv
    queries = projected[:, :channels].astype(jnp.bfloat16)
    key_block = projected[:, channels:2 * channels].astype(jnp.bfloat16)
    values = projected[:, 2 * channels:].astype(jnp.bfloat16)
    score_scale = 1.0 / math.sqrt(channels)
    pixels = frame_rows * frame_cols
    block_rows = math.gcd(pixels, 1024)

    def attend(query_rows):
        scores = jnp.dot(query_rows, key_block.T, preferred_element_type=jnp.float32) * score_scale
        weights = jnp.exp(scores - lax.optimization_barrier(jnp.max(scores, axis=1, keepdims=True)))
        numer = jnp.dot(weights.astype(jnp.bfloat16), values, preferred_element_type=jnp.float32)
        return (numer / lax.optimization_barrier(jnp.sum(weights, axis=1, keepdims=True))).astype(jnp.bfloat16)
    attended = lax.map(attend, queries.reshape(pixels // block_rows, block_rows, channels)).reshape(pixels, channels)
    block_out = middle.astype(jnp.float32) + jnp.dot(attended, w_proj, preferred_element_type=jnp.float32) + b_proj
    return block_out.astype(jnp.bfloat16).reshape(frame_rows, frame_cols, channels)
```

```python
import math

import jax
import jax.numpy as jnp
from jax import lax
from jax.experimental import pallas as pl
from jax.experimental.pallas import tpu as pltpu
from jax.sharding import Mesh
from jax.sharding import PartitionSpec as P

ROW = ("x", "ylo")
COL = ("z", "yhi", "core")
PLANE = ("x", "ylo", "yhi")
C = 384
TILE = 8
PIX = TILE * TILE
QUERIES = 16 * PIX
KEYS = 16 * PIX
SENDS = 4
LANES = 128
BF16 = jnp.bfloat16
F32 = jnp.float32


def pairs(count):
    inner = [(i, i ^ 1) for i in range(count)]
    outer = [(i, ((i + 1) ^ 1) - 1) for i in range(1, count - 1)]
    return inner, outer


def swapped(edges, axes):
    return [lax.ppermute(edge, axes, links) for edge, links in zip(edges, pairs(lax.axis_size(axes)))]


HBM = pl.BlockSpec(memory_space=pltpu.HBM)


def fetch(pairs_in, sems):
    copies = [
        pltpu.make_async_copy(source, target, sems.at[place])
        for place, (source, target) in enumerate(pairs_in)
    ]
    for copy in copies:
        copy.start()
    return copies


def arrive(copies):
    for copy in copies:
        copy.wait()


def row_kernel(cache, hidden, inner, outer, sems):
    odd = lax.axis_index("ylo")
    moves = []
    for edge, row in ((inner, 7 - 7 * odd), (outer, 7 * odd)):
        moves.append((cache.at[:, row], edge.at[pl.ds(0, 2)]))
        moves.append((hidden.at[row], edge.at[2]))
    arrive(fetch(moves, sems))


def row_edges(cache, hidden):
    edge = jax.ShapeDtypeStruct((3, TILE, C), BF16)
    return pl.pallas_call(
        row_kernel,
        in_specs=[HBM, HBM],
        out_shape=[edge, edge],
        scratch_shapes=[pltpu.SemaphoreType.DMA((4,))],
        compiler_params=pltpu.CompilerParams(vmem_limit_bytes=60 << 20),
    )(cache, hidden)


def side_kernel(cache, hidden, sides, wide):
    for frame in range(3):
        own = cache[frame] if frame < 2 else hidden[...]
        wide[frame] = own.astype(F32)
        for place, col in enumerate((0, TILE - 1)):
            sides[place, frame] = wide[frame, :, col, :].astype(BF16)


def own_sides(cache, hidden):
    return pl.pallas_call(
        side_kernel,
        out_shape=jax.ShapeDtypeStruct((2, 3, TILE, C), BF16),
        scratch_shapes=[pltpu.VMEM((3, TILE, TILE, C), F32)],
        compiler_params=pltpu.CompilerParams(vmem_limit_bytes=4 << 20),
        cost_estimate=pl.CostEstimate(flops=1 << 31, bytes_accessed=1 << 20, transcendentals=0),
    )(cache, hidden)


def column_kernel(sides, row_inner, row_outer, inner, outer):
    row_odd = lax.axis_index("ylo")
    odd = lax.axis_index("core")
    for frame in range(3):
        from_inner = row_inner[frame].astype(F32)
        from_outer = row_outer[frame].astype(F32)
        above = jnp.where(row_odd == 1, from_inner, from_outer)
        below = jnp.where(row_odd == 1, from_outer, from_inner)
        left, right = [
            jnp.concatenate(
                [above[col : col + 1], sides[place, frame].astype(F32), below[col : col + 1]], axis=0
            )
            for place, col in enumerate((0, TILE - 1))
        ]
        inner[frame] = jnp.where(odd == 1, left, right).astype(BF16)
        outer[frame] = jnp.where(odd == 1, right, left).astype(BF16)


def column_edges(sides, row_inner, row_outer):
    edge = jax.ShapeDtypeStruct((3, TILE + 2, C), BF16)
    return pl.pallas_call(
        column_kernel,
        out_shape=[edge, edge],
        compiler_params=pltpu.CompilerParams(vmem_limit_bytes=4 << 20),
        cost_estimate=pl.CostEstimate(flops=1 << 34, bytes_accessed=1 << 20, transcendentals=0),
    )(sides, row_inner, row_outer)


def rms(floats, gain):
    return floats * lax.rsqrt(jnp.mean(floats * floats, axis=-1, keepdims=True) + 1e-06) * gain


def conv_kernel(
    cache, hidden, row_inner, row_outer, col_inner, col_outer, weight, skip,
    norm_gain, conv_bias, attn_gain, w_qkv, b_qkv, middle, normed, queries, wide, shifted,
):
    row_odd = lax.axis_index("ylo")
    odd = lax.axis_index("core")
    total = jnp.zeros((PIX, C), F32)
    for frame in range(3):
        own = cache[frame] if frame < 2 else hidden[...]
        wide[pl.ds(1, TILE), 1 : 1 + TILE] = own.astype(F32)
        wide[9 - 9 * row_odd, 1 : 1 + TILE] = row_inner[frame].astype(F32)
        wide[9 * row_odd, 1 : 1 + TILE] = row_outer[frame].astype(F32)
        from_inner = col_inner[frame].astype(F32)
        from_outer = col_outer[frame].astype(F32)
        wide[:, 0] = jnp.where(odd == 1, from_inner, from_outer)
        wide[:, 1 + TILE] = jnp.where(odd == 1, from_outer, from_inner)
        block = wide[:, 0 : TILE + 2]
        if frame == 2:
            block = rms(block, norm_gain[...].reshape(1, 1, C))
            block = (block * jax.nn.sigmoid(block)).astype(BF16).astype(F32)
        for col in range(3):
            shifted[frame, col] = block[:, col : col + TILE, :]
    for frame in range(3):
        for row in range(3):
            tap = 9 * frame + 3 * row
            window = jnp.concatenate(
                [
                    shifted[frame, col, row : row + TILE].reshape(PIX, C).astype(BF16)
                    for col in range(3)
                ],
                axis=1,
            )
            total += jnp.dot(
                window, weight[tap * C : (tap + 3) * C], preferred_element_type=F32
            )
    mid = (skip[...].astype(F32) + (total + conv_bias[...])).astype(BF16)
    middle[...] = mid
    norm = rms(mid.astype(F32), attn_gain[...]).astype(BF16)
    normed[...] = norm
    query = (jnp.dot(norm, w_qkv[:, :C], preferred_element_type=F32) + b_qkv[:C]).astype(BF16)
    for place in range(16):
        queries[place * PIX : (place + 1) * PIX] = query


def conv_stage(cache, hidden, rows, cols, weight, skip, norm_gain, conv_bias, attn_gain, w_qkv, b_qkv):
    out = jax.ShapeDtypeStruct((PIX, C), BF16)
    return pl.pallas_call(
        conv_kernel,
        out_shape=[out, out, jax.ShapeDtypeStruct((QUERIES, C), BF16)],
        scratch_shapes=[
            pltpu.VMEM((TILE + 2, 2 * TILE, C), F32),
            pltpu.VMEM((3, 3, TILE + 2, TILE, C), F32),
        ],
        compiler_params=pltpu.CompilerParams(vmem_limit_bytes=24 << 20),
    )(cache, hidden, *rows, *cols, weight, skip, norm_gain, conv_bias, attn_gain, w_qkv, b_qkv)


def pair_kernel(own, far, both):
    both[:PIX] = own[...]
    both[PIX:] = far[...]


def pair_stage(own, far):
    return pl.pallas_call(
        pair_kernel,
        out_shape=jax.ShapeDtypeStruct((2 * PIX, C), BF16),
        compiler_params=pltpu.CompilerParams(vmem_limit_bytes=4 << 20),
        cost_estimate=pl.CostEstimate(flops=1 << 34, bytes_accessed=1 << 20, transcendentals=0),
    )(own, far)


def split3(value):
    first = value.astype(BF16)
    rest = value - first.astype(F32)
    second = rest.astype(BF16)
    third = (rest - second.astype(F32)).astype(BF16)
    return first.astype(F32), second.astype(F32), third.astype(F32)


def attend_kernel(queries, line, other, w_qkv, b_qkv, partial):
    normed = jnp.concatenate([line[...], other[...]], axis=0)
    projected = jnp.dot(normed, w_qkv[:, C:], preferred_element_type=F32) + b_qkv[C:]
    key_block = projected[:, :C].astype(BF16)
    values = projected[:, C:].astype(BF16).T
    scores = lax.dot_general(
        key_block, queries[...], (((1,), (1,)), ((), ())), preferred_element_type=F32
    ) * (math.log2(math.e) / math.sqrt(C))
    top = jnp.max(scores, axis=0, keepdims=True)
    weights = jnp.exp2(scores - top)
    denom = jnp.sum(weights, axis=0, keepdims=True)
    weights = weights.astype(BF16)
    parts = split3(top) + split3(denom)
    stats = jnp.concatenate(parts + (jnp.zeros((2, QUERIES), F32),), axis=0)
    for place in range(SENDS):
        group = QUERIES // SENDS
        numer = jnp.dot(
            values, weights[:, place * group : (place + 1) * group], preferred_element_type=F32
        ).T.astype(BF16)
        first = place * group // PIX
        for index in range(group // PIX):
            low = (first + index) * PIX
            for part in range(3):
                partial[first + index, part * PIX : (part + 1) * PIX] = numer[
                    index * PIX : (index + 1) * PIX, part * LANES : (part + 1) * LANES
                ]
            partial[first + index, 3 * PIX :] = jnp.concatenate(
                [stats[:, low : low + PIX], jnp.zeros((8, LANES - PIX), F32)], axis=1
            ).astype(BF16)


def attend_stage(queries, line, other, w_qkv, b_qkv):
    return pl.pallas_call(
        attend_kernel,
        out_shape=jax.ShapeDtypeStruct((16, 3 * PIX + 8, LANES), BF16),
        compiler_params=pltpu.CompilerParams(vmem_limit_bytes=40 << 20),
    )(queries, line, other, w_qkv, b_qkv)


def finish_kernel(partials, middle, w_proj, b_proj, block_out):
    stats = partials[:, 3 * PIX :].astype(F32)
    tops = stats[:, 0] + stats[:, 1] + stats[:, 2]
    denoms = stats[:, 3] + stats[:, 4] + stats[:, 5]
    scales = jnp.exp2(tops - jnp.max(tops, axis=0, keepdims=True))
    shares = (scales / jnp.maximum(jnp.sum(scales * denoms, axis=0, keepdims=True), 0.5)).T
    attended = jnp.concatenate(
        [
            sum(
                shares[:PIX, source : source + 1]
                * partials[source, part * PIX : (part + 1) * PIX].astype(F32)
                for source in range(16)
            )
            for part in range(3)
        ],
        axis=1,
    )
    block_out[...] = (
        middle[...].astype(F32)
        + jnp.dot(attended.astype(BF16), w_proj[...], preferred_element_type=F32)
        + b_proj[...]
    ).astype(BF16)


def finish_stage(partials, middle, w_proj, b_proj):
    return pl.pallas_call(
        finish_kernel,
        out_shape=jax.ShapeDtypeStruct((PIX, C), BF16),
        compiler_params=pltpu.CompilerParams(vmem_limit_bytes=8 << 20),
    )(partials, middle, w_proj, b_proj)


def steps(hop, count=8):
    return [(i, (i + hop) % count) for i in range(count)]


def flips(mask, count=8):
    return [(i, i ^ mask) for i in range(count)]


def shards(
    hidden_in,
    skip_input,
    cache_frames,
    norm_gain,
    conv_weight,
    conv_bias,
    attn_gain,
    w_qkv,
    b_qkv,
    w_proj,
    b_proj,
):
    rows = swapped(row_edges(cache_frames, hidden_in), ROW)
    cols = swapped(column_edges(own_sides(cache_frames, hidden_in), *rows), COL)
    middle, normed, queries = conv_stage(
        cache_frames,
        hidden_in,
        rows,
        cols,
        conv_weight.reshape(27 * C, C),
        skip_input.reshape(PIX, C),
        norm_gain,
        conv_bias,
        attn_gain,
        w_qkv,
        b_qkv,
    )
    all_queries = lax.all_to_all(queries, PLANE, 0, 0, tiled=True)
    far = pair_stage(normed, lax.ppermute(normed, "z", flips(4)))
    own_line = jnp.concatenate([far] + [lax.ppermute(far, "z", links) for links in (flips(2), steps(1), steps(-1))], axis=0)
    other_line = lax.ppermute(own_line, "core", flips(1, 2))
    partial = attend_stage(all_queries, own_line, other_line, w_qkv, b_qkv)
    partials = lax.all_to_all(partial, PLANE, 0, 0, tiled=True)
    block_out = finish_stage(partials, middle, w_proj, b_proj)
    return block_out.reshape(TILE, TILE, C)


def solution(mesh):
    fine = Mesh(mesh.devices.reshape(4, 2, 8, 2, 2), ROW + COL)
    return jax.shard_map(
        shards,
        mesh=fine,
        in_specs=(
            P(ROW, COL, None),
            P(ROW, COL, None),
            P(None, ROW, COL, None),
            P(),
            P(),
            P(),
            P(),
            P(),
            P(),
            P(),
            P(),
        ),
        out_specs=P(ROW, COL, None),
        check_vma=False,
    )
```

```python
import math

import jax
import jax.numpy as jnp
from jax import lax
from jax.experimental import pallas as pl
from jax.experimental.pallas import tpu as pltpu
from jax.sharding import Mesh
from jax.sharding import PartitionSpec as P

ROW = ("x", "ylo")
COL = ("z", "yhi", "core")
PLANE = ("x", "yhi", "ylo")
C = 384
TILE = 8
PIX = TILE * TILE
QUERIES = 16 * PIX
KEYS = 16 * PIX
SENDS = 4
LANES = 128
BF16 = jnp.bfloat16
F32 = jnp.float32


def pairs(count):
    inner = [(i, i ^ 1) for i in range(count)]
    outer = [(i, (((i + 1) ^ 1) - 1) % count) for i in range(count)]
    return inner, outer


def swapped(edges, axes):
    inner, outer = pairs(lax.axis_size(axes))
    far = lax.ppermute(edges[1], axes, outer)
    near = lax.ppermute(edges[0], axes, inner)
    return near, far


HBM = pl.BlockSpec(memory_space=pltpu.HBM)


def fetch(pairs_in, sems):
    copies = [
        pltpu.make_async_copy(source, target, sems.at[place])
        for place, (source, target) in enumerate(pairs_in)
    ]
    for copy in copies:
        copy.start()
    return copies


def arrive(copies):
    for copy in copies:
        copy.wait()


def inside_rows(edge):
    place = 2 * lax.axis_index("x") + lax.axis_index("ylo")
    return jnp.where((place == 0) | (place == 7), jnp.zeros_like(edge), edge)


def inside_cols(edge):
    place = 4 * lax.axis_index("z") + 2 * lax.axis_index("yhi") + lax.axis_index("core")
    return jnp.where((place == 0) | (place == 31), jnp.zeros_like(edge), edge)


def row_kernel(cache, hidden, inner, outer, sems):
    odd = lax.axis_index("ylo")
    moves = []
    for edge, row in ((inner, 7 - 7 * odd), (outer, 7 * odd)):
        moves.append((cache.at[:, row], edge.at[pl.ds(0, 2)]))
        moves.append((hidden.at[row], edge.at[2]))
    arrive(fetch(moves, sems))


def row_edges(cache, hidden):
    edge = jax.ShapeDtypeStruct((3, TILE, C), BF16)
    return pl.pallas_call(
        row_kernel,
        in_specs=[HBM, HBM],
        out_shape=[edge, edge],
        scratch_shapes=[pltpu.SemaphoreType.DMA((4,))],
        compiler_params=pltpu.CompilerParams(vmem_limit_bytes=60 << 20),
    )(cache, hidden)


def side_kernel(cache, hidden, sides, wide):
    for frame in range(3):
        own = cache[frame] if frame < 2 else hidden[...]
        wide[frame] = own.astype(F32)
        for place, col in enumerate((0, TILE - 1)):
            sides[place, frame] = wide[frame, :, col, :].astype(BF16)


def own_sides(cache, hidden):
    return pl.pallas_call(
        side_kernel,
        out_shape=jax.ShapeDtypeStruct((2, 3, TILE, C), BF16),
        scratch_shapes=[pltpu.VMEM((3, TILE, TILE, C), F32)],
        compiler_params=pltpu.CompilerParams(vmem_limit_bytes=4 << 20),
        cost_estimate=pl.CostEstimate(flops=1 << 31, bytes_accessed=1 << 20, transcendentals=0),
    )(cache, hidden)


def column_kernel(sides, row_outer, row_inner, inner, outer):
    row_odd = lax.axis_index("ylo")
    odd = lax.axis_index("core")
    for frame in range(3):
        from_inner = row_inner[frame].astype(F32)
        from_outer = inside_rows(row_outer[frame].astype(F32))
        above = jnp.where(row_odd == 1, from_inner, from_outer)
        below = jnp.where(row_odd == 1, from_outer, from_inner)
        left, right = [
            jnp.concatenate(
                [above[col : col + 1], sides[place, frame].astype(F32), below[col : col + 1]], axis=0
            )
            for place, col in enumerate((0, TILE - 1))
        ]
        inner[frame] = jnp.where(odd == 1, left, right).astype(BF16)
        outer[frame] = jnp.where(odd == 1, right, left).astype(BF16)


def column_edges(sides, row_inner, row_outer):
    edge = jax.ShapeDtypeStruct((3, TILE + 2, C), BF16)
    return pl.pallas_call(
        column_kernel,
        out_shape=[edge, edge],
        compiler_params=pltpu.CompilerParams(vmem_limit_bytes=4 << 20),
        cost_estimate=pl.CostEstimate(flops=1 << 34, bytes_accessed=1 << 20, transcendentals=0),
    )(sides, row_outer, row_inner)


def rms(floats, gain):
    return floats * lax.rsqrt(jnp.mean(floats * floats, axis=-1, keepdims=True) + 1e-06) * gain


def conv_kernel(
    cache, hidden, row_outer, row_inner, col_outer, col_inner, weight, skip,
    norm_gain, conv_bias, attn_gain, w_qkv, b_qkv, middle, normed, queries, wide, shifted,
):
    row_odd = lax.axis_index("ylo")
    odd = lax.axis_index("core")
    total = jnp.zeros((PIX, C), F32)
    for frame in range(3):
        own = cache[frame] if frame < 2 else hidden[...]
        wide[pl.ds(1, TILE), 1 : 1 + TILE] = own.astype(F32)
        wide[9 - 9 * row_odd, 1 : 1 + TILE] = row_inner[frame].astype(F32)
        wide[9 * row_odd, 1 : 1 + TILE] = inside_rows(row_outer[frame].astype(F32))
        from_inner = col_inner[frame].astype(F32)
        from_outer = inside_cols(col_outer[frame].astype(F32))
        wide[:, 0] = jnp.where(odd == 1, from_inner, from_outer)
        wide[:, 1 + TILE] = jnp.where(odd == 1, from_outer, from_inner)
        block = wide[:, 0 : TILE + 2]
        if frame == 2:
            block = rms(block, norm_gain[...].reshape(1, 1, C))
            block = (block * jax.nn.sigmoid(block)).astype(BF16).astype(F32)
        for col in range(3):
            shifted[frame, col] = block[:, col : col + TILE, :]
    for frame in range(3):
        for row in range(3):
            tap = 9 * frame + 3 * row
            window = jnp.concatenate(
                [
                    shifted[frame, col, row : row + TILE].reshape(PIX, C).astype(BF16)
                    for col in range(3)
                ],
                axis=1,
            )
            total += jnp.dot(
                window, weight[tap * C : (tap + 3) * C], preferred_element_type=F32
            )
    mid = (skip[...].astype(F32) + (total + conv_bias[...])).astype(BF16)
    middle[...] = mid
    norm = rms(mid.astype(F32), attn_gain[...]).astype(BF16)
    normed[...] = norm
    query = (jnp.dot(norm, w_qkv[:, :C], preferred_element_type=F32) + b_qkv[:C]).astype(BF16)
    for place in range(16):
        queries[place * PIX : (place + 1) * PIX] = query


def conv_stage(cache, hidden, rows, cols, weight, skip, norm_gain, conv_bias, attn_gain, w_qkv, b_qkv):
    out = jax.ShapeDtypeStruct((PIX, C), BF16)
    return pl.pallas_call(
        conv_kernel,
        out_shape=[out, out, jax.ShapeDtypeStruct((QUERIES, C), BF16)],
        scratch_shapes=[
            pltpu.VMEM((TILE + 2, 2 * TILE, C), F32),
            pltpu.VMEM((3, 3, TILE + 2, TILE, C), F32),
        ],
        compiler_params=pltpu.CompilerParams(vmem_limit_bytes=24 << 20),
    )(cache, hidden, *rows[::-1], *cols[::-1], weight, skip, norm_gain, conv_bias, attn_gain, w_qkv, b_qkv)


def pair_kernel(own, far, both):
    both[:PIX] = own[...]
    both[PIX:] = far[...]


def pair_stage(own, far):
    return pl.pallas_call(
        pair_kernel,
        out_shape=jax.ShapeDtypeStruct((2 * PIX, C), BF16),
        compiler_params=pltpu.CompilerParams(vmem_limit_bytes=4 << 20),
        cost_estimate=pl.CostEstimate(flops=1 << 34, bytes_accessed=1 << 20, transcendentals=0),
    )(own, far)


def estimate(flops):
    return pl.CostEstimate(flops=flops, bytes_accessed=1 << 20, transcendentals=0)


def split3(value):
    first = value.astype(BF16)
    rest = value - first.astype(F32)
    second = rest.astype(BF16)
    third = (rest - second.astype(F32)).astype(BF16)
    return first.astype(F32), second.astype(F32), third.astype(F32)


def project_kernel(normed, w_qkv, b_qkv, key_block, values):
    projected = jnp.dot(normed[...], w_qkv[:, C:], preferred_element_type=F32) + b_qkv[C:]
    key_block[...] = projected[:, :C].astype(BF16)
    values[...] = projected[:, C:].astype(BF16).T


def project_stage(normed, w_qkv, b_qkv):
    count = normed.shape[0]
    return pl.pallas_call(
        project_kernel,
        out_shape=[
            jax.ShapeDtypeStruct((count, C), BF16),
            jax.ShapeDtypeStruct((C, count), BF16),
        ],
        compiler_params=pltpu.CompilerParams(vmem_limit_bytes=16 << 20),
        cost_estimate=estimate(1 << 30),
    )(normed, w_qkv, b_qkv)


def attend_kernel(queries, line_keys, line_values, other, w_qkv, b_qkv, partial):
    projected = jnp.dot(other[...], w_qkv[:, C:], preferred_element_type=F32) + b_qkv[C:]
    other_keys = projected[:, :C].astype(BF16)
    other_values = projected[:, C:].astype(BF16).T
    scores = [
        lax.dot_general(
            keys[...], queries[...], (((1,), (1,)), ((), ())), preferred_element_type=F32
        )
        * (math.log2(math.e) / math.sqrt(C))
        for keys in (line_keys, other_keys)
    ]
    top = jnp.maximum(*[jnp.max(part, axis=0, keepdims=True) for part in scores])
    weights = [jnp.exp2(part - top) for part in scores]
    denom = sum(jnp.sum(part, axis=0, keepdims=True) for part in weights)
    weights = jnp.concatenate([part.astype(BF16) for part in weights], axis=0)
    values = jnp.concatenate([line_values[...], other_values], axis=1)
    parts = split3(top) + split3(denom)
    stats = jnp.concatenate(parts + (jnp.zeros((2, QUERIES), F32),), axis=0)
    for place in range(SENDS):
        group = QUERIES // SENDS
        span = slice(place * group, (place + 1) * group)
        numer = jnp.dot(values, weights[:, span], preferred_element_type=F32).T.astype(BF16)
        first = place * group // PIX
        for index in range(group // PIX):
            low = (first + index) * PIX
            for part in range(3):
                partial[first + index, part * PIX : (part + 1) * PIX] = numer[
                    index * PIX : (index + 1) * PIX, part * LANES : (part + 1) * LANES
                ]
            partial[first + index, 3 * PIX :] = jnp.concatenate(
                [stats[:, low : low + PIX], jnp.zeros((8, LANES - PIX), F32)], axis=1
            ).astype(BF16)


def attend_stage(queries, line, other, w_qkv, b_qkv):
    return pl.pallas_call(
        attend_kernel,
        out_shape=jax.ShapeDtypeStruct((16, 3 * PIX + 8, LANES), BF16),
        compiler_params=pltpu.CompilerParams(vmem_limit_bytes=24 << 20),
    )(queries, *line, other, w_qkv, b_qkv)


def finish_kernel(partials, middle, w_proj, b_proj, block_out):
    stats = partials[:, 3 * PIX :].astype(F32)
    tops = stats[:, 0] + stats[:, 1] + stats[:, 2]
    denoms = stats[:, 3] + stats[:, 4] + stats[:, 5]
    scales = jnp.exp2(tops - jnp.max(tops, axis=0, keepdims=True))
    shares = (scales / jnp.maximum(jnp.sum(scales * denoms, axis=0, keepdims=True), 0.5)).T
    attended = jnp.concatenate(
        [
            sum(
                shares[:PIX, source : source + 1]
                * partials[source, part * PIX : (part + 1) * PIX].astype(F32)
                for source in range(16)
            )
            for part in range(3)
        ],
        axis=1,
    )
    block_out[...] = (
        middle[...].astype(F32)
        + jnp.dot(attended.astype(BF16), w_proj[...], preferred_element_type=F32)
        + b_proj[...]
    ).astype(BF16)


def finish_stage(partials, middle, w_proj, b_proj):
    return pl.pallas_call(
        finish_kernel,
        out_shape=jax.ShapeDtypeStruct((PIX, C), BF16),
        compiler_params=pltpu.CompilerParams(vmem_limit_bytes=8 << 20),
    )(partials, middle, w_proj, b_proj)


def steps(hop, count=8):
    return [(i, (i + hop) % count) for i in range(count)]


def flips(mask, count=8):
    return [(i, i ^ mask) for i in range(count)]


def shards(
    hidden_in,
    skip_input,
    cache_frames,
    norm_gain,
    conv_weight,
    conv_bias,
    attn_gain,
    w_qkv,
    b_qkv,
    w_proj,
    b_proj,
):
    rows = swapped(row_edges(cache_frames, hidden_in), ROW)
    cols = swapped(column_edges(own_sides(cache_frames, hidden_in), *rows), COL)
    middle, normed, queries = conv_stage(
        cache_frames,
        hidden_in,
        rows,
        cols,
        conv_weight.reshape(27 * C, C),
        skip_input.reshape(PIX, C),
        norm_gain,
        conv_bias,
        attn_gain,
        w_qkv,
        b_qkv,
    )
    all_queries = lax.all_to_all(queries, PLANE, 0, 0, tiled=True)
    far = pair_stage(normed, lax.ppermute(normed, "z", flips(4)))
    own_line = jnp.concatenate([far] + [lax.ppermute(far, "z", links) for links in (steps(1), steps(-1), flips(2))], axis=0)
    other_line = lax.ppermute(own_line, "core", flips(1, 2))
    partial = attend_stage(
        all_queries,
        project_stage(own_line, w_qkv, b_qkv),
        other_line,
        w_qkv,
        b_qkv,
    )
    partials = lax.all_to_all(partial, PLANE, 0, 0, tiled=True)
    block_out = finish_stage(partials, middle, w_proj, b_proj)
    return block_out.reshape(TILE, TILE, C)


def solution(mesh):
    fine = Mesh(mesh.devices.reshape(4, 2, 8, 2, 2), ROW + COL)
    return jax.shard_map(
        shards,
        mesh=fine,
        in_specs=(
            P(ROW, COL, None),
            P(ROW, COL, None),
            P(None, ROW, COL, None),
            P(),
            P(),
            P(),
            P(),
            P(),
            P(),
            P(),
            P(),
        ),
        out_specs=P(ROW, COL, None),
        check_vma=False,
    )
```

```python
import math

import jax
import jax.numpy as jnp
from jax import lax
from jax.experimental import pallas as pl
from jax.experimental.pallas import tpu as pltpu
from jax.sharding import Mesh
from jax.sharding import PartitionSpec as P

ROW = ("x", "ylo")
COL = ("z", "yhi", "core")
PLANE = ("x", "yhi", "ylo")
C = 384
TILE = 8
PIX = TILE * TILE
QUERIES = 16 * PIX
KEYS = 16 * PIX
SENDS = 4
LANES = 128
BF16 = jnp.bfloat16
F32 = jnp.float32


def pairs(count):
    inner = [(i, i ^ 1) for i in range(count)]
    outer = [(i, (((i + 1) ^ 1) - 1) % count) for i in range(count)]
    return inner, outer


def swapped(edges, axes):
    inner, outer = pairs(lax.axis_size(axes))
    far = lax.ppermute(edges[1], axes, outer)
    near = lax.ppermute(edges[0], axes, inner)
    return near, far


HBM = pl.BlockSpec(memory_space=pltpu.HBM)


def fetch(pairs_in, sems):
    copies = [
        pltpu.make_async_copy(source, target, sems.at[place])
        for place, (source, target) in enumerate(pairs_in)
    ]
    for copy in copies:
        copy.start()
    return copies


def arrive(copies):
    for copy in copies:
        copy.wait()


def inside_rows(edge):
    place = 2 * lax.axis_index("x") + lax.axis_index("ylo")
    return jnp.where((place == 0) | (place == 7), jnp.zeros_like(edge), edge)


def inside_cols(edge):
    place = 4 * lax.axis_index("z") + 2 * lax.axis_index("yhi") + lax.axis_index("core")
    return jnp.where((place == 0) | (place == 31), jnp.zeros_like(edge), edge)


def edge_kernel(cache_h, hidden_h, outer, inner, sides, cache, hidden, wide, sems):
    odd = lax.axis_index("ylo")
    arrive(fetch(((cache_h, cache), (hidden_h, hidden)), sems))
    for frame in range(3):
        own = (cache[frame] if frame < 2 else hidden[...]).astype(F32)
        wide[...] = own
        outer[frame] = jnp.where(odd == 1, own[TILE - 1], own[0]).astype(BF16)
        inner[frame] = jnp.where(odd == 1, own[0], own[TILE - 1]).astype(BF16)
        for place, col in enumerate((0, TILE - 1)):
            sides[place, frame] = wide[:, col, :].astype(BF16)


def own_edges(cache, hidden):
    edge = jax.ShapeDtypeStruct((3, TILE, C), BF16)
    outer, inner, sides = pl.pallas_call(
        edge_kernel,
        in_specs=[HBM, HBM],
        out_shape=[edge, edge, jax.ShapeDtypeStruct((2, 3, TILE, C), BF16)],
        scratch_shapes=[
            pltpu.VMEM((2, TILE, TILE, C), BF16),
            pltpu.VMEM((TILE, TILE, C), BF16),
            pltpu.VMEM((TILE, TILE, C), F32),
            pltpu.SemaphoreType.DMA((2,)),
        ],
        compiler_params=pltpu.CompilerParams(vmem_limit_bytes=55120 << 10),
    )(cache, hidden)
    return (inner, outer), sides


def column_kernel(sides, row_outer, row_inner, inner, outer):
    row_odd = lax.axis_index("ylo")
    odd = lax.axis_index("core")
    for frame in range(3):
        from_inner = row_inner[frame].astype(F32)
        from_outer = inside_rows(row_outer[frame].astype(F32))
        above = jnp.where(row_odd == 1, from_inner, from_outer)
        below = jnp.where(row_odd == 1, from_outer, from_inner)
        left, right = [
            jnp.concatenate(
                [above[col : col + 1], sides[place, frame].astype(F32), below[col : col + 1]], axis=0
            )
            for place, col in enumerate((0, TILE - 1))
        ]
        inner[frame] = jnp.where(odd == 1, left, right).astype(BF16)
        outer[frame] = jnp.where(odd == 1, right, left).astype(BF16)


def column_edges(sides, row_inner, row_outer):
    edge = jax.ShapeDtypeStruct((3, TILE + 2, C), BF16)
    return pl.pallas_call(
        column_kernel,
        out_shape=[edge, edge],
        compiler_params=pltpu.CompilerParams(vmem_limit_bytes=4 << 20),
        cost_estimate=pl.CostEstimate(flops=1 << 34, bytes_accessed=1 << 20, transcendentals=0),
    )(sides, row_outer, row_inner)


def rms(floats, gain):
    return floats * lax.rsqrt(jnp.mean(floats * floats, axis=-1, keepdims=True) + 1e-06) * gain


def conv_kernel(
    cache, hidden, row_outer, row_inner, col_outer, col_inner, weight, skip,
    norm_gain, conv_bias, attn_gain, w_qkv, b_qkv, middle, normed, queries, wide, shifted,
):
    row_odd = lax.axis_index("ylo")
    odd = lax.axis_index("core")
    total = jnp.zeros((PIX, C), F32)
    for frame in range(3):
        own = cache[frame] if frame < 2 else hidden[...]
        wide[pl.ds(1, TILE), 1 : 1 + TILE] = own.astype(F32)
        wide[9 - 9 * row_odd, 1 : 1 + TILE] = row_inner[frame].astype(F32)
        wide[9 * row_odd, 1 : 1 + TILE] = inside_rows(row_outer[frame].astype(F32))
        from_inner = col_inner[frame].astype(F32)
        from_outer = inside_cols(col_outer[frame].astype(F32))
        wide[:, 0] = jnp.where(odd == 1, from_inner, from_outer)
        wide[:, 1 + TILE] = jnp.where(odd == 1, from_outer, from_inner)
        block = wide[:, 0 : TILE + 2]
        if frame == 2:
            block = rms(block, norm_gain[...].reshape(1, 1, C))
            block = (block * jax.nn.sigmoid(block)).astype(BF16).astype(F32)
        for col in range(3):
            shifted[frame, col] = block[:, col : col + TILE, :]
    for frame in range(3):
        for row in range(3):
            tap = 9 * frame + 3 * row
            window = jnp.concatenate(
                [
                    shifted[frame, col, row : row + TILE].reshape(PIX, C).astype(BF16)
                    for col in range(3)
                ],
                axis=1,
            )
            total += jnp.dot(
                window, weight[tap * C : (tap + 3) * C], preferred_element_type=F32
            )
    mid = (skip[...].astype(F32) + (total + conv_bias[...])).astype(BF16)
    middle[...] = mid
    norm = rms(mid.astype(F32), attn_gain[...]).astype(BF16)
    normed[...] = norm
    query = (jnp.dot(norm, w_qkv[:, :C], preferred_element_type=F32) + b_qkv[:C]).astype(BF16)
    for place in range(16):
        queries[place * PIX : (place + 1) * PIX] = query


def conv_stage(cache, hidden, rows, cols, weight, skip, norm_gain, conv_bias, attn_gain, w_qkv, b_qkv):
    out = jax.ShapeDtypeStruct((PIX, C), BF16)
    return pl.pallas_call(
        conv_kernel,
        out_shape=[out, out, jax.ShapeDtypeStruct((QUERIES, C), BF16)],
        scratch_shapes=[
            pltpu.VMEM((TILE + 2, 2 * TILE, C), F32),
            pltpu.VMEM((3, 3, TILE + 2, TILE, C), F32),
        ],
        compiler_params=pltpu.CompilerParams(vmem_limit_bytes=24 << 20),
    )(cache, hidden, *rows[::-1], *cols[::-1], weight, skip, norm_gain, conv_bias, attn_gain, w_qkv, b_qkv)


def pair_kernel(own, far, both):
    both[:PIX] = own[...]
    both[PIX:] = far[...]


def pair_stage(own, far):
    return pl.pallas_call(
        pair_kernel,
        out_shape=jax.ShapeDtypeStruct((2 * PIX, C), BF16),
        compiler_params=pltpu.CompilerParams(vmem_limit_bytes=4 << 20),
        cost_estimate=pl.CostEstimate(flops=1 << 34, bytes_accessed=1 << 20, transcendentals=0),
    )(own, far)


def estimate(flops):
    return pl.CostEstimate(flops=flops, bytes_accessed=1 << 20, transcendentals=0)


def split3(value):
    first = value.astype(BF16)
    rest = value - first.astype(F32)
    second = rest.astype(BF16)
    third = (rest - second.astype(F32)).astype(BF16)
    return first.astype(F32), second.astype(F32), third.astype(F32)


def project_kernel(normed, w_qkv, b_qkv, key_block, values):
    projected = jnp.dot(normed[...], w_qkv[:, C:], preferred_element_type=F32) + b_qkv[C:]
    key_block[...] = projected[:, :C].astype(BF16)
    values[...] = projected[:, C:].astype(BF16).T


def project_stage(normed, w_qkv, b_qkv):
    count = normed.shape[0]
    return pl.pallas_call(
        project_kernel,
        out_shape=[
            jax.ShapeDtypeStruct((count, C), BF16),
            jax.ShapeDtypeStruct((C, count), BF16),
        ],
        compiler_params=pltpu.CompilerParams(vmem_limit_bytes=16 << 20),
        cost_estimate=estimate(1 << 30),
    )(normed, w_qkv, b_qkv)


def attend_kernel(queries, line_keys, line_values, other, w_qkv, b_qkv, partial):
    projected = jnp.dot(other[...], w_qkv[:, C:], preferred_element_type=F32) + b_qkv[C:]
    other_keys = projected[:, :C].astype(BF16)
    other_values = projected[:, C:].astype(BF16).T
    scores = [
        lax.dot_general(
            keys[...], queries[...], (((1,), (1,)), ((), ())), preferred_element_type=F32
        )
        * (math.log2(math.e) / math.sqrt(C))
        for keys in (line_keys, other_keys)
    ]
    top = jnp.maximum(*[jnp.max(part, axis=0, keepdims=True) for part in scores])
    weights = [jnp.exp2(part - top) for part in scores]
    denom = sum(jnp.sum(part, axis=0, keepdims=True) for part in weights)
    weights = jnp.concatenate([part.astype(BF16) for part in weights], axis=0)
    values = jnp.concatenate([line_values[...], other_values], axis=1)
    parts = split3(top) + split3(denom)
    stats = jnp.concatenate(parts + (jnp.zeros((2, QUERIES), F32),), axis=0)
    for place in range(SENDS):
        group = QUERIES // SENDS
        span = slice(place * group, (place + 1) * group)
        numer = jnp.dot(values, weights[:, span], preferred_element_type=F32).T.astype(BF16)
        first = place * group // PIX
        for index in range(group // PIX):
            low = (first + index) * PIX
            for part in range(3):
                partial[first + index, part * PIX : (part + 1) * PIX] = numer[
                    index * PIX : (index + 1) * PIX, part * LANES : (part + 1) * LANES
                ]
            partial[first + index, 3 * PIX :] = jnp.concatenate(
                [stats[:, low : low + PIX], jnp.zeros((8, LANES - PIX), F32)], axis=1
            ).astype(BF16)


def attend_stage(queries, line, other, w_qkv, b_qkv):
    return pl.pallas_call(
        attend_kernel,
        out_shape=jax.ShapeDtypeStruct((16, 3 * PIX + 8, LANES), BF16),
        compiler_params=pltpu.CompilerParams(vmem_limit_bytes=24 << 20),
    )(queries, *line, other, w_qkv, b_qkv)


def finish_kernel(partials, middle, w_proj, b_proj, block_out):
    stats = partials[:, 3 * PIX :].astype(F32)
    tops = stats[:, 0] + stats[:, 1] + stats[:, 2]
    denoms = stats[:, 3] + stats[:, 4] + stats[:, 5]
    scales = jnp.exp2(tops - jnp.max(tops, axis=0, keepdims=True))
    shares = (scales / jnp.maximum(jnp.sum(scales * denoms, axis=0, keepdims=True), 0.5)).T
    attended = jnp.concatenate(
        [
            sum(
                shares[:PIX, source : source + 1]
                * partials[source, part * PIX : (part + 1) * PIX].astype(F32)
                for source in range(16)
            )
            for part in range(3)
        ],
        axis=1,
    )
    block_out[...] = (
        middle[...].astype(F32)
        + jnp.dot(attended.astype(BF16), w_proj[...], preferred_element_type=F32)
        + b_proj[...]
    ).astype(BF16)


def finish_stage(partials, middle, w_proj, b_proj):
    return pl.pallas_call(
        finish_kernel,
        out_shape=jax.ShapeDtypeStruct((PIX, C), BF16),
        compiler_params=pltpu.CompilerParams(vmem_limit_bytes=8 << 20),
    )(partials, middle, w_proj, b_proj)


def steps(hop, count=8):
    return [(i, (i + hop) % count) for i in range(count)]


def flips(mask, count=8):
    return [(i, i ^ mask) for i in range(count)]


def shards(
    hidden_in,
    skip_input,
    cache_frames,
    norm_gain,
    conv_weight,
    conv_bias,
    attn_gain,
    w_qkv,
    b_qkv,
    w_proj,
    b_proj,
):
    edges, own_sides = own_edges(cache_frames, hidden_in)
    rows = swapped(edges, ROW)
    cols = swapped(column_edges(own_sides, *rows), COL)
    middle, normed, queries = conv_stage(
        cache_frames,
        hidden_in,
        rows,
        cols,
        conv_weight.reshape(27 * C, C),
        skip_input.reshape(PIX, C),
        norm_gain,
        conv_bias,
        attn_gain,
        w_qkv,
        b_qkv,
    )
    all_queries = lax.all_to_all(queries, PLANE, 0, 0, tiled=True)
    far = pair_stage(normed, lax.ppermute(normed, "z", flips(4)))
    own_line = jnp.concatenate([far] + [lax.ppermute(far, "z", links) for links in (steps(1), steps(-1), flips(2))], axis=0)
    other_line = lax.ppermute(own_line, "core", flips(1, 2))
    partial = attend_stage(
        all_queries,
        project_stage(own_line, w_qkv, b_qkv),
        other_line,
        w_qkv,
        b_qkv,
    )
    partials = lax.all_to_all(partial, PLANE, 0, 0, tiled=True)
    block_out = finish_stage(partials, middle, w_proj, b_proj)
    return block_out.reshape(TILE, TILE, C)


def solution(mesh):
    fine = Mesh(mesh.devices.reshape(4, 2, 8, 2, 2), ROW + COL)
    return jax.shard_map(
        shards,
        mesh=fine,
        in_specs=(
            P(ROW, COL, None),
            P(ROW, COL, None),
            P(None, ROW, COL, None),
            P(),
            P(),
            P(),
            P(),
            P(),
            P(),
            P(),
            P(),
        ),
        out_specs=P(ROW, COL, None),
        check_vma=False,
    )
```

```python
import math

import jax
import jax.numpy as jnp
from jax import lax
from jax.experimental import pallas as pl
from jax.experimental.pallas import tpu as pltpu
from jax.sharding import Mesh
from jax.sharding import PartitionSpec as P

ROW = ("x", "ylo")
COL = ("z", "yhi", "core")
PLANE = ("x", "yhi", "ylo")
C = 384
TILE = 8
PIX = TILE * TILE
QUERIES = 16 * PIX
KEYS = 16 * PIX
SENDS = 4
LANES = 128
BF16 = jnp.bfloat16
F32 = jnp.float32


def pairs(count):
    inner = [(i, i ^ 1) for i in range(count)]
    outer = [(i, (((i + 1) ^ 1) - 1) % count) for i in range(count)]
    return inner, outer


def swapped(edges, axes):
    inner, outer = pairs(lax.axis_size(axes))
    far = lax.ppermute(edges[1], axes, outer)
    near = lax.ppermute(edges[0], axes, inner)
    return near, far


HBM = pl.BlockSpec(memory_space=pltpu.HBM)


def fetch(pairs_in, sems):
    copies = [
        pltpu.make_async_copy(source, target, sems.at[place])
        for place, (source, target) in enumerate(pairs_in)
    ]
    for copy in copies:
        copy.start()
    return copies


def arrive(copies):
    for copy in copies:
        copy.wait()


def inside_rows(edge):
    place = 2 * lax.axis_index("x") + lax.axis_index("ylo")
    return jnp.where((place == 0) | (place == 7), jnp.zeros_like(edge), edge)


def inside_cols(edge):
    place = 4 * lax.axis_index("z") + 2 * lax.axis_index("yhi") + lax.axis_index("core")
    return jnp.where((place == 0) | (place == 31), jnp.zeros_like(edge), edge)


def edge_kernel(cache_h, hidden_h, outer, inner, sides, cache, hidden, wide, sems):
    odd = lax.axis_index("ylo")
    arrive(fetch(((cache_h, cache), (hidden_h, hidden)), sems))
    for frame in range(3):
        own = (cache[frame] if frame < 2 else hidden[...]).astype(F32)
        wide[...] = own
        outer[frame] = jnp.where(odd == 1, own[TILE - 1], own[0]).astype(BF16)
        inner[frame] = jnp.where(odd == 1, own[0], own[TILE - 1]).astype(BF16)
        for place, col in enumerate((0, TILE - 1)):
            sides[place, frame] = wide[:, col, :].astype(BF16)


def own_edges(cache, hidden):
    edge = jax.ShapeDtypeStruct((3, TILE, C), BF16)
    outer, inner, sides = pl.pallas_call(
        edge_kernel,
        in_specs=[HBM, HBM],
        out_shape=[edge, edge, jax.ShapeDtypeStruct((2, 3, TILE, C), BF16)],
        scratch_shapes=[
            pltpu.VMEM((2, TILE, TILE, C), BF16),
            pltpu.VMEM((TILE, TILE, C), BF16),
            pltpu.VMEM((TILE, TILE, C), F32),
            pltpu.SemaphoreType.DMA((2,)),
        ],
        compiler_params=pltpu.CompilerParams(vmem_limit_bytes=55120 << 10),
    )(cache, hidden)
    return (inner, outer), sides


def column_kernel(sides, row_outer, row_inner, inner, outer):
    row_odd = lax.axis_index("ylo")
    odd = lax.axis_index("core")
    for frame in range(3):
        from_inner = row_inner[frame].astype(F32)
        from_outer = inside_rows(row_outer[frame].astype(F32))
        above = jnp.where(row_odd == 1, from_inner, from_outer)
        below = jnp.where(row_odd == 1, from_outer, from_inner)
        left, right = [
            jnp.concatenate(
                [above[col : col + 1], sides[place, frame].astype(F32), below[col : col + 1]], axis=0
            )
            for place, col in enumerate((0, TILE - 1))
        ]
        inner[frame] = jnp.where(odd == 1, left, right).astype(BF16)
        outer[frame] = jnp.where(odd == 1, right, left).astype(BF16)


def column_edges(sides, row_inner, row_outer):
    edge = jax.ShapeDtypeStruct((3, TILE + 2, C), BF16)
    return pl.pallas_call(
        column_kernel,
        out_shape=[edge, edge],
        compiler_params=pltpu.CompilerParams(vmem_limit_bytes=4 << 20),
        cost_estimate=pl.CostEstimate(flops=1 << 34, bytes_accessed=1 << 20, transcendentals=0),
    )(sides, row_outer, row_inner)


def rms(floats, gain):
    return floats * lax.rsqrt(jnp.mean(floats * floats, axis=-1, keepdims=True) + 1e-06) * gain


def conv_input(block, gain):
    block = rms(block, gain)
    return (block * jax.nn.sigmoid(block)).astype(BF16).astype(F32)


def tap(rows, weight, frame, row, col):
    start = (9 * frame + 3 * row + col) * C
    return jnp.dot(
        rows[row : row + TILE].reshape(PIX, C).astype(BF16),
        weight[start : start + C],
        preferred_element_type=F32,
    )


def centre_kernel(cache, hidden, row_outer, row_inner, weight, norm_gain, total, tall):
    odd = lax.axis_index("ylo")
    partial = jnp.zeros((PIX, C), F32)
    for frame in range(3):
        from_inner = row_inner[frame].astype(F32)
        from_outer = inside_rows(row_outer[frame].astype(F32))
        above = jnp.where(odd == 1, from_inner, from_outer)
        below = jnp.where(odd == 1, from_outer, from_inner)
        own = (cache[frame] if frame < 2 else hidden[...]).astype(F32)
        block = jnp.concatenate([above[None], own, below[None]], axis=0)
        if frame == 2:
            block = conv_input(block, norm_gain[...].reshape(1, 1, C))
        tall[frame] = block
        for row in range(3):
            partial += tap(block, weight, frame, row, 1)
    total[...] = partial


def centre_stage(cache, hidden, rows, weight, norm_gain):
    return pl.pallas_call(
        centre_kernel,
        out_shape=[
            jax.ShapeDtypeStruct((PIX, C), F32),
            jax.ShapeDtypeStruct((3, TILE + 2, TILE, C), F32),
        ],
        compiler_params=pltpu.CompilerParams(vmem_limit_bytes=16 << 20),
        cost_estimate=pl.CostEstimate(flops=1 << 31, bytes_accessed=1 << 20, transcendentals=0),
    )(cache, hidden, *rows[::-1], weight, norm_gain)


def conv_kernel(
    centre, tall, col_outer, col_inner, weight, skip,
    norm_gain, conv_bias, attn_gain, w_qkv, b_qkv, middle, normed, queries, wide,
):
    odd = lax.axis_index("core")
    total = centre[...]
    for frame in range(3):
        from_inner = col_inner[frame].astype(F32)
        from_outer = inside_cols(col_outer[frame].astype(F32))
        left = jnp.where(odd == 1, from_inner, from_outer)
        right = jnp.where(odd == 1, from_outer, from_inner)
        if frame == 2:
            left, right = conv_input(left, norm_gain[...]), conv_input(right, norm_gain[...])
        wide[:, 1 : 1 + TILE] = tall[frame]
        wide[:, 0] = left
        wide[:, 1 + TILE] = right
        for col in (0, 2):
            block = wide[:, col : col + TILE]
            for row in range(3):
                total += tap(block, weight, frame, row, col)
    mid = (skip[...].astype(F32) + (total + conv_bias[...])).astype(BF16)
    middle[...] = mid
    norm = rms(mid.astype(F32), attn_gain[...]).astype(BF16)
    normed[...] = norm
    query = (jnp.dot(norm, w_qkv[:, :C], preferred_element_type=F32) + b_qkv[:C]).astype(BF16)
    for place in range(16):
        queries[place * PIX : (place + 1) * PIX] = query


def conv_stage(centre, cols, weight, skip, norm_gain, conv_bias, attn_gain, w_qkv, b_qkv):
    out = jax.ShapeDtypeStruct((PIX, C), BF16)
    return pl.pallas_call(
        conv_kernel,
        out_shape=[out, out, jax.ShapeDtypeStruct((QUERIES, C), BF16)],
        scratch_shapes=[pltpu.VMEM((TILE + 2, 2 * TILE, C), F32)],
        compiler_params=pltpu.CompilerParams(vmem_limit_bytes=24 << 20),
    )(*centre, *cols[::-1], weight, skip, norm_gain, conv_bias, attn_gain, w_qkv, b_qkv)


def pair_kernel(own, far, both):
    both[:PIX] = own[...]
    both[PIX:] = far[...]


def pair_stage(own, far):
    return pl.pallas_call(
        pair_kernel,
        out_shape=jax.ShapeDtypeStruct((2 * PIX, C), BF16),
        compiler_params=pltpu.CompilerParams(vmem_limit_bytes=4 << 20),
        cost_estimate=pl.CostEstimate(flops=1 << 34, bytes_accessed=1 << 20, transcendentals=0),
    )(own, far)


def estimate(flops):
    return pl.CostEstimate(flops=flops, bytes_accessed=1 << 20, transcendentals=0)


def split3(value):
    first = value.astype(BF16)
    rest = value - first.astype(F32)
    second = rest.astype(BF16)
    third = (rest - second.astype(F32)).astype(BF16)
    return first.astype(F32), second.astype(F32), third.astype(F32)


def project_kernel(normed, w_qkv, b_qkv, key_block, values):
    projected = jnp.dot(normed[...], w_qkv[:, C:], preferred_element_type=F32) + b_qkv[C:]
    key_block[...] = projected[:, :C].astype(BF16)
    values[...] = projected[:, C:].astype(BF16).T


def project_stage(normed, w_qkv, b_qkv):
    count = normed.shape[0]
    return pl.pallas_call(
        project_kernel,
        out_shape=[
            jax.ShapeDtypeStruct((count, C), BF16),
            jax.ShapeDtypeStruct((C, count), BF16),
        ],
        compiler_params=pltpu.CompilerParams(vmem_limit_bytes=16 << 20),
        cost_estimate=estimate(1 << 30),
    )(normed, w_qkv, b_qkv)


def attend_kernel(queries, line_keys, line_values, other, w_qkv, b_qkv, partial):
    projected = jnp.dot(other[...], w_qkv[:, C:], preferred_element_type=F32) + b_qkv[C:]
    other_keys = projected[:, :C].astype(BF16)
    other_values = projected[:, C:].astype(BF16).T
    scores = [
        lax.dot_general(
            keys[...], queries[...], (((1,), (1,)), ((), ())), preferred_element_type=F32
        )
        * (math.log2(math.e) / math.sqrt(C))
        for keys in (line_keys, other_keys)
    ]
    top = jnp.maximum(*[jnp.max(part, axis=0, keepdims=True) for part in scores])
    weights = [jnp.exp2(part - top) for part in scores]
    denom = sum(jnp.sum(part, axis=0, keepdims=True) for part in weights)
    weights = jnp.concatenate([part.astype(BF16) for part in weights], axis=0)
    values = jnp.concatenate([line_values[...], other_values], axis=1)
    parts = split3(top) + split3(denom)
    stats = jnp.concatenate(parts + (jnp.zeros((2, QUERIES), F32),), axis=0)
    for place in range(SENDS):
        group = QUERIES // SENDS
        span = slice(place * group, (place + 1) * group)
        numer = jnp.dot(values, weights[:, span], preferred_element_type=F32).T.astype(BF16)
        first = place * group // PIX
        for index in range(group // PIX):
            low = (first + index) * PIX
            for part in range(3):
                partial[first + index, part * PIX : (part + 1) * PIX] = numer[
                    index * PIX : (index + 1) * PIX, part * LANES : (part + 1) * LANES
                ]
            partial[first + index, 3 * PIX :] = jnp.concatenate(
                [stats[:, low : low + PIX], jnp.zeros((8, LANES - PIX), F32)], axis=1
            ).astype(BF16)


def attend_stage(queries, line, other, w_qkv, b_qkv):
    return pl.pallas_call(
        attend_kernel,
        out_shape=jax.ShapeDtypeStruct((16, 3 * PIX + 8, LANES), BF16),
        compiler_params=pltpu.CompilerParams(vmem_limit_bytes=24 << 20),
    )(queries, *line, other, w_qkv, b_qkv)


def finish_kernel(partials, middle, w_proj, b_proj, block_out):
    stats = partials[:, 3 * PIX :].astype(F32)
    tops = stats[:, 0] + stats[:, 1] + stats[:, 2]
    denoms = stats[:, 3] + stats[:, 4] + stats[:, 5]
    scales = jnp.exp2(tops - jnp.max(tops, axis=0, keepdims=True))
    shares = (scales / jnp.maximum(jnp.sum(scales * denoms, axis=0, keepdims=True), 0.5)).T
    attended = jnp.concatenate(
        [
            sum(
                shares[:PIX, source : source + 1]
                * partials[source, part * PIX : (part + 1) * PIX].astype(F32)
                for source in range(16)
            )
            for part in range(3)
        ],
        axis=1,
    )
    block_out[...] = (
        middle[...].astype(F32)
        + jnp.dot(attended.astype(BF16), w_proj[...], preferred_element_type=F32)
        + b_proj[...]
    ).astype(BF16)


def finish_stage(partials, middle, w_proj, b_proj):
    return pl.pallas_call(
        finish_kernel,
        out_shape=jax.ShapeDtypeStruct((PIX, C), BF16),
        compiler_params=pltpu.CompilerParams(vmem_limit_bytes=8 << 20),
    )(partials, middle, w_proj, b_proj)


def steps(hop, count=8):
    return [(i, (i + hop) % count) for i in range(count)]


def flips(mask, count=8):
    return [(i, i ^ mask) for i in range(count)]


def shards(
    hidden_in,
    skip_input,
    cache_frames,
    norm_gain,
    conv_weight,
    conv_bias,
    attn_gain,
    w_qkv,
    b_qkv,
    w_proj,
    b_proj,
):
    edges, own_sides = own_edges(cache_frames, hidden_in)
    rows = swapped(edges, ROW)
    cols = swapped(column_edges(own_sides, *rows), COL)
    weight = conv_weight.reshape(27 * C, C)
    middle, normed, queries = conv_stage(
        centre_stage(cache_frames, hidden_in, rows, weight, norm_gain),
        cols,
        weight,
        skip_input.reshape(PIX, C),
        norm_gain,
        conv_bias,
        attn_gain,
        w_qkv,
        b_qkv,
    )
    all_queries = lax.all_to_all(queries, PLANE, 0, 0, tiled=True)
    far = pair_stage(normed, lax.ppermute(normed, "z", flips(4)))
    own_line = jnp.concatenate([far] + [lax.ppermute(far, "z", links) for links in (steps(1), steps(-1), flips(2))], axis=0)
    other_line = lax.ppermute(own_line, "core", flips(1, 2))
    partial = attend_stage(
        all_queries,
        project_stage(own_line, w_qkv, b_qkv),
        other_line,
        w_qkv,
        b_qkv,
    )
    partials = lax.all_to_all(partial, PLANE, 0, 0, tiled=True)
    block_out = finish_stage(partials, middle, w_proj, b_proj)
    return block_out.reshape(TILE, TILE, C)


def solution(mesh):
    fine = Mesh(mesh.devices.reshape(4, 2, 8, 2, 2), ROW + COL)
    return jax.shard_map(
        shards,
        mesh=fine,
        in_specs=(
            P(ROW, COL, None),
            P(ROW, COL, None),
            P(None, ROW, COL, None),
            P(),
            P(),
            P(),
            P(),
            P(),
            P(),
            P(),
            P(),
        ),
        out_specs=P(ROW, COL, None),
        check_vma=False,
    )
```

```python
import math

import jax
import jax.numpy as jnp
from jax import lax
from jax.experimental import pallas as pl
from jax.experimental.pallas import tpu as pltpu
from jax.sharding import Mesh
from jax.sharding import PartitionSpec as P

ROW = ("x", "ylo")
COL = ("z", "yhi", "core")
PLANE = ("x", "yhi", "ylo")
C = 384
TILE = 8
PIX = TILE * TILE
QUERIES = 16 * PIX
KEYS = 16 * PIX
SENDS = 4
LANES = 128
BF16 = jnp.bfloat16
F32 = jnp.float32


def pairs(count):
    inner = [(i, i ^ 1) for i in range(count)]
    outer = [(i, (((i + 1) ^ 1) - 1) % count) for i in range(count)]
    return inner, outer


def swapped(edges, axes):
    inner, outer = pairs(lax.axis_size(axes))
    far = lax.ppermute(edges[1], axes, outer)
    near = lax.ppermute(edges[0], axes, inner)
    return near, far


HBM = pl.BlockSpec(memory_space=pltpu.HBM)


def fetch(pairs_in, sems):
    copies = [
        pltpu.make_async_copy(source, target, sems.at[place])
        for place, (source, target) in enumerate(pairs_in)
    ]
    for copy in copies:
        copy.start()
    return copies


def arrive(copies):
    for copy in copies:
        copy.wait()


def inside_rows(edge):
    place = 2 * lax.axis_index("x") + lax.axis_index("ylo")
    return jnp.where((place == 0) | (place == 7), jnp.zeros_like(edge), edge)


def inside_cols(edge):
    place = 4 * lax.axis_index("z") + 2 * lax.axis_index("yhi") + lax.axis_index("core")
    return jnp.where((place == 0) | (place == 31), jnp.zeros_like(edge), edge)


def edge_kernel(cache_h, hidden_h, outer, inner, sides, cache, hidden, wide, sems):
    odd = lax.axis_index("ylo")
    arrive(fetch(((cache_h, cache), (hidden_h, hidden)), sems))
    for frame in range(3):
        own = (cache[frame] if frame < 2 else hidden[...]).astype(F32)
        wide[...] = own
        outer[frame] = jnp.where(odd == 1, own[TILE - 1], own[0]).astype(BF16)
        inner[frame] = jnp.where(odd == 1, own[0], own[TILE - 1]).astype(BF16)
        for place, col in enumerate((0, TILE - 1)):
            sides[place, frame] = wide[:, col, :].astype(BF16)


def own_edges(cache, hidden):
    edge = jax.ShapeDtypeStruct((3, TILE, C), BF16)
    outer, inner, sides = pl.pallas_call(
        edge_kernel,
        in_specs=[HBM, HBM],
        out_shape=[edge, edge, jax.ShapeDtypeStruct((2, 3, TILE, C), BF16)],
        scratch_shapes=[
            pltpu.VMEM((2, TILE, TILE, C), BF16),
            pltpu.VMEM((TILE, TILE, C), BF16),
            pltpu.VMEM((TILE, TILE, C), F32),
            pltpu.SemaphoreType.DMA((2,)),
        ],
        compiler_params=pltpu.CompilerParams(vmem_limit_bytes=55120 << 10),
    )(cache, hidden)
    return (inner, outer), sides


def column_kernel(sides, row_outer, row_inner, inner, outer):
    row_odd = lax.axis_index("ylo")
    odd = lax.axis_index("core")
    for frame in range(3):
        from_inner = row_inner[frame].astype(F32)
        from_outer = inside_rows(row_outer[frame].astype(F32))
        above = jnp.where(row_odd == 1, from_inner, from_outer)
        below = jnp.where(row_odd == 1, from_outer, from_inner)
        left, right = [
            jnp.concatenate(
                [above[col : col + 1], sides[place, frame].astype(F32), below[col : col + 1]], axis=0
            )
            for place, col in enumerate((0, TILE - 1))
        ]
        inner[frame] = jnp.where(odd == 1, left, right).astype(BF16)
        outer[frame] = jnp.where(odd == 1, right, left).astype(BF16)


def column_edges(sides, row_inner, row_outer):
    edge = jax.ShapeDtypeStruct((3, TILE + 2, C), BF16)
    return pl.pallas_call(
        column_kernel,
        out_shape=[edge, edge],
        compiler_params=pltpu.CompilerParams(vmem_limit_bytes=4 << 20),
        cost_estimate=pl.CostEstimate(flops=1 << 34, bytes_accessed=1 << 20, transcendentals=0),
    )(sides, row_outer, row_inner)


def rms(floats, gain):
    return floats * lax.rsqrt(jnp.mean(floats * floats, axis=-1, keepdims=True) + 1e-06) * gain


def conv_input(block, gain):
    block = rms(block, gain)
    return (block * jax.nn.sigmoid(block)).astype(BF16).astype(F32)


def tap(rows, weight, frame, row, col):
    start = (9 * frame + 3 * row + col) * C
    return jnp.dot(
        rows[row : row + TILE].reshape(PIX, C).astype(BF16),
        weight[start : start + C],
        preferred_element_type=F32,
    )


def centre_kernel(cache, hidden, row_outer, row_inner, weight, norm_gain, total, tall):
    odd = lax.axis_index("ylo")
    partial = jnp.zeros((PIX, C), F32)
    for frame in range(3):
        from_inner = row_inner[frame].astype(F32)
        from_outer = inside_rows(row_outer[frame].astype(F32))
        above = jnp.where(odd == 1, from_inner, from_outer)
        below = jnp.where(odd == 1, from_outer, from_inner)
        own = (cache[frame] if frame < 2 else hidden[...]).astype(F32)
        block = jnp.concatenate([above[None], own, below[None]], axis=0)
        if frame == 2:
            block = conv_input(block, norm_gain[...].reshape(1, 1, C))
        tall[frame] = block
        for row in range(3):
            partial += tap(block, weight, frame, row, 1)
    total[...] = partial


def centre_stage(cache, hidden, rows, weight, norm_gain):
    return pl.pallas_call(
        centre_kernel,
        out_shape=[
            jax.ShapeDtypeStruct((PIX, C), F32),
            jax.ShapeDtypeStruct((3, TILE + 2, TILE, C), F32),
        ],
        compiler_params=pltpu.CompilerParams(vmem_limit_bytes=16 << 20),
        cost_estimate=pl.CostEstimate(flops=1 << 31, bytes_accessed=1 << 20, transcendentals=0),
    )(cache, hidden, *rows[::-1], weight, norm_gain)


def conv_kernel(
    centre, tall, col_outer, col_inner, weight, skip,
    norm_gain, conv_bias, attn_gain, w_qkv, b_qkv, middle, normed, queries, wide,
):
    odd = lax.axis_index("core")
    total = centre[...]
    windows = []
    for frame in range(3):
        from_inner = col_inner[frame].astype(F32)
        from_outer = inside_cols(col_outer[frame].astype(F32))
        left = jnp.where(odd == 1, from_inner, from_outer)
        right = jnp.where(odd == 1, from_outer, from_inner)
        if frame == 2:
            left, right = conv_input(left, norm_gain[...]), conv_input(right, norm_gain[...])
        wide[:, 1 : 1 + TILE] = tall[frame]
        wide[:, 0] = left
        wide[:, 1 + TILE] = right
        blocks = [wide[:, col : col + TILE] for col in (0, 2)]
        for row in range(3):
            for col, block in zip((0, 2), blocks):
                window = block[row : row + TILE].reshape(PIX, C).astype(BF16)
                windows.append((9 * frame + 3 * row + col, window))
    for group in [windows[:1]] + [windows[i : i + 2] for i in range(1, len(windows), 2)]:
        start = group[0][0] * C
        total += jnp.dot(
            jnp.concatenate([window for _, window in group], axis=1),
            weight[start : start + len(group) * C],
            preferred_element_type=F32,
        )
    mid = (skip[...].astype(F32) + (total + conv_bias[...])).astype(BF16)
    middle[...] = mid
    norm = rms(mid.astype(F32), attn_gain[...]).astype(BF16)
    normed[...] = norm
    query = (jnp.dot(norm, w_qkv[:, :C], preferred_element_type=F32) + b_qkv[:C]).astype(BF16)
    for place in range(16):
        queries[place * PIX : (place + 1) * PIX] = query


def conv_stage(centre, cols, weight, skip, norm_gain, conv_bias, attn_gain, w_qkv, b_qkv):
    out = jax.ShapeDtypeStruct((PIX, C), BF16)
    return pl.pallas_call(
        conv_kernel,
        out_shape=[out, out, jax.ShapeDtypeStruct((QUERIES, C), BF16)],
        scratch_shapes=[pltpu.VMEM((TILE + 2, 2 * TILE, C), F32)],
        compiler_params=pltpu.CompilerParams(vmem_limit_bytes=24 << 20),
    )(*centre, *cols[::-1], weight, skip, norm_gain, conv_bias, attn_gain, w_qkv, b_qkv)


def pair_kernel(own, far, both):
    both[:PIX] = own[...]
    both[PIX:] = far[...]


def pair_stage(own, far):
    return pl.pallas_call(
        pair_kernel,
        out_shape=jax.ShapeDtypeStruct((2 * PIX, C), BF16),
        compiler_params=pltpu.CompilerParams(vmem_limit_bytes=4 << 20),
        cost_estimate=pl.CostEstimate(flops=1 << 34, bytes_accessed=1 << 20, transcendentals=0),
    )(own, far)


def estimate(flops):
    return pl.CostEstimate(flops=flops, bytes_accessed=1 << 20, transcendentals=0)


def split3(value):
    first = value.astype(BF16)
    rest = value - first.astype(F32)
    second = rest.astype(BF16)
    third = (rest - second.astype(F32)).astype(BF16)
    return first.astype(F32), second.astype(F32), third.astype(F32)


def project_kernel(normed, w_qkv, b_qkv, key_block, values):
    projected = jnp.dot(normed[...], w_qkv[:, C:], preferred_element_type=F32) + b_qkv[C:]
    key_block[...] = projected[:, :C].astype(BF16)
    values[...] = projected[:, C:].astype(BF16).T


def project_stage(normed, w_qkv, b_qkv):
    count = normed.shape[0]
    return pl.pallas_call(
        project_kernel,
        out_shape=[
            jax.ShapeDtypeStruct((count, C), BF16),
            jax.ShapeDtypeStruct((C, count), BF16),
        ],
        compiler_params=pltpu.CompilerParams(vmem_limit_bytes=16 << 20),
        cost_estimate=estimate(1 << 30),
    )(normed, w_qkv, b_qkv)


def attend_kernel(queries, line_keys, line_values, other, w_qkv, b_qkv, partial):
    projected = jnp.dot(other[...], w_qkv[:, C:], preferred_element_type=F32) + b_qkv[C:]
    other_keys = projected[:, :C].astype(BF16)
    other_values = projected[:, C:].astype(BF16).T
    scores = [
        lax.dot_general(
            keys[...], queries[...], (((1,), (1,)), ((), ())), preferred_element_type=F32
        )
        * (math.log2(math.e) / math.sqrt(C))
        for keys in (line_keys, other_keys)
    ]
    top = jnp.maximum(*[jnp.max(part, axis=0, keepdims=True) for part in scores])
    weights = [jnp.exp2(part - top) for part in scores]
    denom = sum(jnp.sum(part, axis=0, keepdims=True) for part in weights)
    weights = jnp.concatenate([part.astype(BF16) for part in weights], axis=0)
    values = jnp.concatenate([line_values[...], other_values], axis=1)
    parts = split3(top) + split3(denom)
    stats = jnp.concatenate(parts + (jnp.zeros((2, QUERIES), F32),), axis=0)
    for place in range(SENDS):
        group = QUERIES // SENDS
        span = slice(place * group, (place + 1) * group)
        numer = jnp.dot(values, weights[:, span], preferred_element_type=F32).T.astype(BF16)
        first = place * group // PIX
        for index in range(group // PIX):
            low = (first + index) * PIX
            for part in range(3):
                partial[first + index, part * PIX : (part + 1) * PIX] = numer[
                    index * PIX : (index + 1) * PIX, part * LANES : (part + 1) * LANES
                ]
            partial[first + index, 3 * PIX :] = jnp.concatenate(
                [stats[:, low : low + PIX], jnp.zeros((8, LANES - PIX), F32)], axis=1
            ).astype(BF16)


def attend_stage(queries, line, other, w_qkv, b_qkv):
    return pl.pallas_call(
        attend_kernel,
        out_shape=jax.ShapeDtypeStruct((16, 3 * PIX + 8, LANES), BF16),
        compiler_params=pltpu.CompilerParams(vmem_limit_bytes=24 << 20),
    )(queries, *line, other, w_qkv, b_qkv)


def finish_kernel(partials, middle, w_proj, b_proj, block_out):
    stats = partials[:, 3 * PIX :].astype(F32)
    tops = stats[:, 0] + stats[:, 1] + stats[:, 2]
    denoms = stats[:, 3] + stats[:, 4] + stats[:, 5]
    scales = jnp.exp2(tops - jnp.max(tops, axis=0, keepdims=True))
    shares = (scales / jnp.maximum(jnp.sum(scales * denoms, axis=0, keepdims=True), 0.5)).T
    attended = jnp.concatenate(
        [
            sum(
                shares[:PIX, source : source + 1]
                * partials[source, part * PIX : (part + 1) * PIX].astype(F32)
                for source in range(16)
            )
            for part in range(3)
        ],
        axis=1,
    )
    block_out[...] = (
        middle[...].astype(F32)
        + jnp.dot(attended.astype(BF16), w_proj[...], preferred_element_type=F32)
        + b_proj[...]
    ).astype(BF16)


def finish_stage(partials, middle, w_proj, b_proj):
    return pl.pallas_call(
        finish_kernel,
        out_shape=jax.ShapeDtypeStruct((PIX, C), BF16),
        compiler_params=pltpu.CompilerParams(vmem_limit_bytes=8 << 20),
    )(partials, middle, w_proj, b_proj)


def steps(hop, count=8):
    return [(i, (i + hop) % count) for i in range(count)]


def flips(mask, count=8):
    return [(i, i ^ mask) for i in range(count)]


def shards(
    hidden_in,
    skip_input,
    cache_frames,
    norm_gain,
    conv_weight,
    conv_bias,
    attn_gain,
    w_qkv,
    b_qkv,
    w_proj,
    b_proj,
):
    edges, own_sides = own_edges(cache_frames, hidden_in)
    rows = swapped(edges, ROW)
    cols = swapped(column_edges(own_sides, *rows), COL)
    weight = conv_weight.reshape(27 * C, C)
    middle, normed, queries = conv_stage(
        centre_stage(cache_frames, hidden_in, rows, weight, norm_gain),
        cols,
        weight,
        skip_input.reshape(PIX, C),
        norm_gain,
        conv_bias,
        attn_gain,
        w_qkv,
        b_qkv,
    )
    all_queries = lax.all_to_all(queries, PLANE, 0, 0, tiled=True)
    far = pair_stage(normed, lax.ppermute(normed, "z", flips(4)))
    own_line = jnp.concatenate([far] + [lax.ppermute(far, "z", links) for links in (steps(1), steps(-1), flips(2))], axis=0)
    other_line = lax.ppermute(own_line, "core", flips(1, 2))
    partial = attend_stage(
        all_queries,
        project_stage(own_line, w_qkv, b_qkv),
        other_line,
        w_qkv,
        b_qkv,
    )
    partials = lax.all_to_all(partial, PLANE, 0, 0, tiled=True)
    block_out = finish_stage(partials, middle, w_proj, b_proj)
    return block_out.reshape(TILE, TILE, C)


def solution(mesh):
    fine = Mesh(mesh.devices.reshape(4, 2, 8, 2, 2), ROW + COL)
    return jax.shard_map(
        shards,
        mesh=fine,
        in_specs=(
            P(ROW, COL, None),
            P(ROW, COL, None),
            P(None, ROW, COL, None),
            P(),
            P(),
            P(),
            P(),
            P(),
            P(),
            P(),
            P(),
        ),
        out_specs=P(ROW, COL, None),
        check_vma=False,
    )
```

```python
import math

import jax
import jax.numpy as jnp
from jax import lax
from jax.experimental import pallas as pl
from jax.experimental.pallas import tpu as pltpu
from jax.sharding import Mesh
from jax.sharding import PartitionSpec as P

ROW = ("x", "ylo")
COL = ("z", "yhi", "core")
PLANE = ("x", "yhi", "ylo")
C = 384
TILE = 8
PIX = TILE * TILE
QUERIES = 16 * PIX
KEYS = 16 * PIX
SENDS = 4
LANES = 128
BF16 = jnp.bfloat16
F32 = jnp.float32


def pairs(count):
    inner = [(i, i ^ 1) for i in range(count)]
    outer = [(i, (((i + 1) ^ 1) - 1) % count) for i in range(count)]
    return inner, outer


def swapped(edges, axes):
    inner, outer = pairs(lax.axis_size(axes))
    far = lax.ppermute(edges[1], axes, outer)
    near = lax.ppermute(edges[0], axes, inner)
    return near, far


HBM = pl.BlockSpec(memory_space=pltpu.HBM)


def fetch(pairs_in, sems):
    copies = [
        pltpu.make_async_copy(source, target, sems.at[place])
        for place, (source, target) in enumerate(pairs_in)
    ]
    for copy in copies:
        copy.start()
    return copies


def arrive(copies):
    for copy in copies:
        copy.wait()


def inside_rows(edge):
    place = 2 * lax.axis_index("x") + lax.axis_index("ylo")
    return jnp.where((place == 0) | (place == 7), jnp.zeros_like(edge), edge)


def inside_cols(edge):
    place = 4 * lax.axis_index("z") + 2 * lax.axis_index("yhi") + lax.axis_index("core")
    return jnp.where((place == 0) | (place == 31), jnp.zeros_like(edge), edge)


def edge_kernel(cache_h, hidden_h, outer, inner, sides, cache, hidden, wide, sems):
    odd = lax.axis_index("ylo")
    arriving = fetch(
        ((cache_h.at[0], cache.at[0]), (cache_h.at[1], cache.at[1]), (hidden_h, hidden)), sems
    )
    for frame in range(3):
        arriving[frame].wait()
        own = (cache[frame] if frame < 2 else hidden[...]).astype(F32)
        wide[...] = own
        outer[frame] = jnp.where(odd == 1, own[TILE - 1], own[0]).astype(BF16)
        inner[frame] = jnp.where(odd == 1, own[0], own[TILE - 1]).astype(BF16)
        for place, col in enumerate((0, TILE - 1)):
            sides[place, frame] = wide[:, col, :].astype(BF16)


def own_edges(cache, hidden):
    edge = jax.ShapeDtypeStruct((3, TILE, C), BF16)
    outer, inner, sides = pl.pallas_call(
        edge_kernel,
        in_specs=[HBM, HBM],
        out_shape=[edge, edge, jax.ShapeDtypeStruct((2, 3, TILE, C), BF16)],
        scratch_shapes=[
            pltpu.VMEM((2, TILE, TILE, C), BF16),
            pltpu.VMEM((TILE, TILE, C), BF16),
            pltpu.VMEM((TILE, TILE, C), F32),
            pltpu.SemaphoreType.DMA((3,)),
        ],
        compiler_params=pltpu.CompilerParams(vmem_limit_bytes=55120 << 10),
    )(cache, hidden)
    return (inner, outer), sides


def column_kernel(sides, row_outer, row_inner, inner, outer):
    row_odd = lax.axis_index("ylo")
    odd = lax.axis_index("core")
    for frame in range(3):
        from_inner = row_inner[frame].astype(F32)
        from_outer = inside_rows(row_outer[frame].astype(F32))
        above = jnp.where(row_odd == 1, from_inner, from_outer)
        below = jnp.where(row_odd == 1, from_outer, from_inner)
        left, right = [
            jnp.concatenate(
                [above[col : col + 1], sides[place, frame].astype(F32), below[col : col + 1]], axis=0
            )
            for place, col in enumerate((0, TILE - 1))
        ]
        inner[frame] = jnp.where(odd == 1, left, right).astype(BF16)
        outer[frame] = jnp.where(odd == 1, right, left).astype(BF16)


def column_edges(sides, row_inner, row_outer):
    edge = jax.ShapeDtypeStruct((3, TILE + 2, C), BF16)
    return pl.pallas_call(
        column_kernel,
        out_shape=[edge, edge],
        compiler_params=pltpu.CompilerParams(vmem_limit_bytes=4 << 20),
        cost_estimate=pl.CostEstimate(flops=1 << 34, bytes_accessed=1 << 20, transcendentals=0),
    )(sides, row_outer, row_inner)


def rms(floats, gain):
    return floats * lax.rsqrt(jnp.mean(floats * floats, axis=-1, keepdims=True) + 1e-06) * gain


def conv_input(block, gain):
    block = rms(block, gain)
    return (block * jax.nn.sigmoid(block)).astype(BF16).astype(F32)


def tap(rows, weight, frame, row, col):
    start = (9 * frame + 3 * row + col) * C
    return jnp.dot(
        rows[row : row + TILE].reshape(PIX, C).astype(BF16),
        weight[start : start + C],
        preferred_element_type=F32,
    )


def centre_kernel(cache, hidden, row_outer, row_inner, weight, norm_gain, total, tall):
    odd = lax.axis_index("ylo")
    partial = jnp.zeros((PIX, C), F32)
    for frame in range(3):
        from_inner = row_inner[frame].astype(F32)
        from_outer = inside_rows(row_outer[frame].astype(F32))
        above = jnp.where(odd == 1, from_inner, from_outer)
        below = jnp.where(odd == 1, from_outer, from_inner)
        own = (cache[frame] if frame < 2 else hidden[...]).astype(F32)
        block = jnp.concatenate([above[None], own, below[None]], axis=0)
        if frame == 2:
            block = conv_input(block, norm_gain[...].reshape(1, 1, C))
        tall[frame] = block
        for row in range(3):
            partial += tap(block, weight, frame, row, 1)
    total[...] = partial


def centre_stage(cache, hidden, rows, weight, norm_gain):
    return pl.pallas_call(
        centre_kernel,
        out_shape=[
            jax.ShapeDtypeStruct((PIX, C), F32),
            jax.ShapeDtypeStruct((3, TILE + 2, TILE, C), F32),
        ],
        compiler_params=pltpu.CompilerParams(vmem_limit_bytes=16 << 20),
        cost_estimate=pl.CostEstimate(flops=1 << 31, bytes_accessed=1 << 20, transcendentals=0),
    )(cache, hidden, *rows[::-1], weight, norm_gain)


def conv_kernel(
    centre, tall, col_outer, col_inner, weight, skip,
    norm_gain, conv_bias, attn_gain, w_qkv, b_qkv, middle, normed, queries, wide,
):
    odd = lax.axis_index("core")
    total = centre[...]
    windows = []
    for frame in range(3):
        from_inner = col_inner[frame].astype(F32)
        from_outer = inside_cols(col_outer[frame].astype(F32))
        left = jnp.where(odd == 1, from_inner, from_outer)
        right = jnp.where(odd == 1, from_outer, from_inner)
        if frame == 2:
            left, right = conv_input(left, norm_gain[...]), conv_input(right, norm_gain[...])
        wide[:, 1 : 1 + TILE] = tall[frame]
        wide[:, 0] = left
        wide[:, 1 + TILE] = right
        blocks = [wide[:, col : col + TILE] for col in (0, 2)]
        for row in range(3):
            for col, block in zip((0, 2), blocks):
                window = block[row : row + TILE].reshape(PIX, C).astype(BF16)
                windows.append((9 * frame + 3 * row + col, window))
    for group in [windows[:1]] + [windows[i : i + 2] for i in range(1, len(windows), 2)]:
        start = group[0][0] * C
        total += jnp.dot(
            jnp.concatenate([window for _, window in group], axis=1),
            weight[start : start + len(group) * C],
            preferred_element_type=F32,
        )
    mid = (skip[...].astype(F32) + (total + conv_bias[...])).astype(BF16)
    middle[...] = mid
    norm = rms(mid.astype(F32), attn_gain[...]).astype(BF16)
    normed[...] = norm
    query = (jnp.dot(norm, w_qkv[:, :C], preferred_element_type=F32) + b_qkv[:C]).astype(BF16)
    for place in range(16):
        queries[place * PIX : (place + 1) * PIX] = query


def conv_stage(centre, cols, weight, skip, norm_gain, conv_bias, attn_gain, w_qkv, b_qkv):
    out = jax.ShapeDtypeStruct((PIX, C), BF16)
    return pl.pallas_call(
        conv_kernel,
        out_shape=[out, out, jax.ShapeDtypeStruct((QUERIES, C), BF16)],
        scratch_shapes=[pltpu.VMEM((TILE + 2, 2 * TILE, C), F32)],
        compiler_params=pltpu.CompilerParams(vmem_limit_bytes=24 << 20),
    )(*centre, *cols[::-1], weight, skip, norm_gain, conv_bias, attn_gain, w_qkv, b_qkv)


def pair_kernel(own, far, both):
    both[:PIX] = own[...]
    both[PIX:] = far[...]


def pair_stage(own, far):
    return pl.pallas_call(
        pair_kernel,
        out_shape=jax.ShapeDtypeStruct((2 * PIX, C), BF16),
        compiler_params=pltpu.CompilerParams(vmem_limit_bytes=4 << 20),
        cost_estimate=pl.CostEstimate(flops=1 << 34, bytes_accessed=1 << 20, transcendentals=0),
    )(own, far)


def estimate(flops):
    return pl.CostEstimate(flops=flops, bytes_accessed=1 << 20, transcendentals=0)


def split3(value):
    first = value.astype(BF16)
    rest = value - first.astype(F32)
    second = rest.astype(BF16)
    third = (rest - second.astype(F32)).astype(BF16)
    return first.astype(F32), second.astype(F32), third.astype(F32)


def project_kernel(normed, w_qkv, b_qkv, key_block, values):
    projected = jnp.dot(normed[...], w_qkv[:, C:], preferred_element_type=F32) + b_qkv[C:]
    key_block[...] = projected[:, :C].astype(BF16)
    values[...] = projected[:, C:].astype(BF16).T


def project_stage(normed, w_qkv, b_qkv):
    count = normed.shape[0]
    return pl.pallas_call(
        project_kernel,
        out_shape=[
            jax.ShapeDtypeStruct((count, C), BF16),
            jax.ShapeDtypeStruct((C, count), BF16),
        ],
        compiler_params=pltpu.CompilerParams(vmem_limit_bytes=16 << 20),
        cost_estimate=estimate(1 << 30),
    )(normed, w_qkv, b_qkv)


def attend_kernel(queries, line_keys, line_values, other, w_qkv, b_qkv, partial):
    projected = jnp.dot(other[...], w_qkv[:, C:], preferred_element_type=F32) + b_qkv[C:]
    other_keys = projected[:, :C].astype(BF16)
    other_values = projected[:, C:].astype(BF16).T
    scores = [
        lax.dot_general(
            keys[...], queries[...], (((1,), (1,)), ((), ())), preferred_element_type=F32
        )
        * (math.log2(math.e) / math.sqrt(C))
        for keys in (line_keys, other_keys)
    ]
    top = jnp.maximum(*[jnp.max(part, axis=0, keepdims=True) for part in scores])
    weights = [jnp.exp2(part - top) for part in scores]
    denom = sum(jnp.sum(part, axis=0, keepdims=True) for part in weights)
    weights = jnp.concatenate([part.astype(BF16) for part in weights], axis=0)
    values = jnp.concatenate([line_values[...], other_values], axis=1)
    parts = split3(top) + split3(denom)
    stats = jnp.concatenate(parts + (jnp.zeros((2, QUERIES), F32),), axis=0)
    for place in range(SENDS):
        group = QUERIES // SENDS
        span = slice(place * group, (place + 1) * group)
        numer = jnp.dot(values, weights[:, span], preferred_element_type=F32).T.astype(BF16)
        first = place * group // PIX
        for index in range(group // PIX):
            low = (first + index) * PIX
            for part in range(3):
                partial[first + index, part * PIX : (part + 1) * PIX] = numer[
                    index * PIX : (index + 1) * PIX, part * LANES : (part + 1) * LANES
                ]
            partial[first + index, 3 * PIX :] = jnp.concatenate(
                [stats[:, low : low + PIX], jnp.zeros((8, LANES - PIX), F32)], axis=1
            ).astype(BF16)


def attend_stage(queries, line, other, w_qkv, b_qkv):
    return pl.pallas_call(
        attend_kernel,
        out_shape=jax.ShapeDtypeStruct((16, 3 * PIX + 8, LANES), BF16),
        compiler_params=pltpu.CompilerParams(vmem_limit_bytes=24 << 20),
    )(queries, *line, other, w_qkv, b_qkv)


def finish_kernel(partials, middle, w_proj, b_proj, block_out):
    stats = partials[:, 3 * PIX :].astype(F32)
    tops = stats[:, 0] + stats[:, 1] + stats[:, 2]
    denoms = stats[:, 3] + stats[:, 4] + stats[:, 5]
    scales = jnp.exp2(tops - jnp.max(tops, axis=0, keepdims=True))
    shares = (scales / jnp.maximum(jnp.sum(scales * denoms, axis=0, keepdims=True), 0.5)).T
    attended = jnp.concatenate(
        [
            sum(
                shares[:PIX, source : source + 1]
                * partials[source, part * PIX : (part + 1) * PIX].astype(F32)
                for source in range(16)
            )
            for part in range(3)
        ],
        axis=1,
    )
    block_out[...] = (
        middle[...].astype(F32)
        + jnp.dot(attended.astype(BF16), w_proj[...], preferred_element_type=F32)
        + b_proj[...]
    ).astype(BF16)


def finish_stage(partials, middle, w_proj, b_proj):
    return pl.pallas_call(
        finish_kernel,
        out_shape=jax.ShapeDtypeStruct((PIX, C), BF16),
        compiler_params=pltpu.CompilerParams(vmem_limit_bytes=8 << 20),
    )(partials, middle, w_proj, b_proj)


def steps(hop, count=8):
    return [(i, (i + hop) % count) for i in range(count)]


def flips(mask, count=8):
    return [(i, i ^ mask) for i in range(count)]


def shards(
    hidden_in,
    skip_input,
    cache_frames,
    norm_gain,
    conv_weight,
    conv_bias,
    attn_gain,
    w_qkv,
    b_qkv,
    w_proj,
    b_proj,
):
    edges, own_sides = own_edges(cache_frames, hidden_in)
    rows = swapped(edges, ROW)
    cols = swapped(column_edges(own_sides, *rows), COL)
    weight = conv_weight.reshape(27 * C, C)
    middle, normed, queries = conv_stage(
        centre_stage(cache_frames, hidden_in, rows, weight, norm_gain),
        cols,
        weight,
        skip_input.reshape(PIX, C),
        norm_gain,
        conv_bias,
        attn_gain,
        w_qkv,
        b_qkv,
    )
    all_queries = lax.all_to_all(queries, PLANE, 0, 0, tiled=True)
    far = pair_stage(normed, lax.ppermute(normed, "z", flips(4)))
    own_line = jnp.concatenate([far] + [lax.ppermute(far, "z", links) for links in (steps(1), steps(-1), flips(2))], axis=0)
    other_line = lax.ppermute(own_line, "core", flips(1, 2))
    partial = attend_stage(
        all_queries,
        project_stage(own_line, w_qkv, b_qkv),
        other_line,
        w_qkv,
        b_qkv,
    )
    partials = lax.all_to_all(partial, PLANE, 0, 0, tiled=True)
    block_out = finish_stage(partials, middle, w_proj, b_proj)
    return block_out.reshape(TILE, TILE, C)


def solution(mesh):
    fine = Mesh(mesh.devices.reshape(4, 2, 8, 2, 2), ROW + COL)
    return jax.shard_map(
        shards,
        mesh=fine,
        in_specs=(
            P(ROW, COL, None),
            P(ROW, COL, None),
            P(None, ROW, COL, None),
            P(),
            P(),
            P(),
            P(),
            P(),
            P(),
            P(),
            P(),
        ),
        out_specs=P(ROW, COL, None),
        check_vma=False,
    )
```
